32 devices in a mesh: expert: 8 (over z, y), context: 2 (over x), dp: 2 (over core).
Axes of the slice: x: 2, y: 2, z: 4, core: 2. Of those that a mesh axis runs over, the one named last changes fastest.
Arguments:
- tokens: bfloat16 [16, 1024, 768], P(('expert', 'dp'), 'context'), may hold values from -6 to 6
- gain_one: float32 [768], replicated, may hold values from 0.1 to 1.9
- w_qkv: bfloat16 [768, 2304], replicated, may hold values from -0.21875 to 0.21875
- w_out: bfloat16 [768, 768], replicated, may hold values from -6 to 6
- gain_two: float32 [768], replicated, may hold values from 0.1 to 1.9
- w_router: bfloat16 [768, 8], replicated, may hold values from -0.15625 to 0.15625
- w_in: bfloat16 [8, 768, 3072], P('expert'), may hold values from -0.21875 to 0.21875
- w_back: bfloat16 [8, 3072, 768], P('expert'), may hold values from -1.75 to 1.75
- expert_ids: int32 [2, 16, 512, 2], P('context', ('expert', 'dp')), may hold values from 0 to 7, all different within a row; in each aligned block of 512 rows (0 to 511, 512 to 1023, ..., all dimensions but the last counted through in order) at most 256 rows name the same one
- cotangent: bfloat16 [16, 1024, 768], P(('expert', 'dp'), 'context'), may hold values from -6 to 6
Outputs:
- output: bfloat16 [16, 1024, 768], P(('expert', 'dp'), 'context')
- grad_tokens: float32 [16, 1024, 768], P(('expert', 'dp'), 'context')
- grad_gain_one: float32 [768], replicated
- grad_qkv: float32 [768, 2304], replicated
- grad_out: float32 [768, 768], replicated
- grad_gain_two: float32 [768], replicated
- grad_router: float32 [768, 8], replicated
- grad_in: float32 [8, 768, 3072], P('expert', ('context', 'dp'))
- grad_back: float32 [8, 3072, 768], P('expert', ('context', 'dp'))
The draws below stay inside these ranges and needn't reach their ends.
Inputs may be any that keep to these rules, and one draw needn't show every extreme that they name: `expert_ids`: each token names 2 different experts, numbered by the owner's index along expert. Within the 512 rows of one device (its images of one context index, image by image, in order) no expert is named more than 256 times.
All inputs are finite; a program needn't handle non-finite values.
Results may differ from the reference program's by a relative error of at most 0.017.
Values may be sent and summed in bfloat16 or wider, within the bound.
A program may use at most 256 MiB of HBM per device.

```python
import math
import jax
import jax.numpy as jnp
import numpy as np
from jax import lax

D = 768
HEADS = 12
HEAD_DIM = 64
FF = 3072
TOPK = 2
SEQ = 1024
TOK_DEV = 512
TOK_CTX = 512
IMG_DEV = 1
IMAGES = 16
EXPERTS = 8
CAP = 256
N_EXPERT = 8
N_CONTEXT = 2


def level_of(key, extent, pieces, least, largest):
    level = 1.0
    for dim, shards_of in pieces:
        draws = jax.random.uniform(jax.random.fold_in(jax.random.fold_in(key, 6), dim), (shards_of,), jnp.float32, least / len(pieces), largest / len(pieces))
        level = level * jnp.repeat(jnp.exp(draws), extent[dim] // shards_of).reshape((-1,) + (1,) * (len(extent) - 1 - dim))
    return level


def assign_block(key, own, number, rows, amount, top, reach, slope):
    order = jax.random.permutation(key, amount)
    crowded, ordinary = portions_of(amount, rows * top, reach, slope, True), portions_of(amount, rows * top, reach, slope, False)
    places = jnp.arange(amount)

    def named(lengths, offset_by):
        used = int((lengths > 0).sum())
        fixed = max(1, used // 4)
        moved = fixed + (places - fixed + offset_by * (used - fixed)) % max(1, amount - fixed)
        return jnp.zeros((amount,), jnp.int32).at[order[jnp.where(places < fixed, places, moved)]].set(jnp.asarray(lengths, jnp.int32))

    lengths = jnp.where(number % 4 == 0, named(crowded, number // 4), named(ordinary, number - number // 4 - 1))
    mixed = jax.random.permutation(jax.random.fold_in(own, 3), amount)
    giver, receiver = mixed[0:amount // 2 * 2:2], mixed[1:amount // 2 * 2:2]
    margin = jnp.minimum(lengths[giver] - 1, reach - lengths[receiver]) // 2
    margin = jnp.where((giver == order[0]) | (receiver == order[0]) | (lengths[receiver] == 0), 0, jnp.maximum(margin, 0))
    moved = jax.random.randint(jax.random.fold_in(own, 4), (amount // 2,), 0, 1 << 20) % (margin + 1)
    lengths = lengths.at[giver].add(-moved).at[receiver].add(moved)
    items = jnp.searchsorted(jnp.cumsum(lengths), jnp.arange(rows * top), side="right").astype(jnp.int32)
    table = items.reshape(top, rows).T
    table = table[jax.random.permutation(jax.random.fold_in(own, 1), rows)]
    offset_by = jax.random.randint(jax.random.fold_in(own, 2), (rows, 1), 0, top)
    return jnp.take_along_axis(table, (jnp.arange(top)[None, :] + offset_by) % top, axis=1)


def portions_of(count, total, limit, skew, full):
    loads = [(1 << 20) // math.isqrt(rank ** skew) + 1 for rank in range(1, count + 1)]
    largest = limit if full else min(limit, max(-(-total // count), total * loads[0] // sum(loads)))
    least = 1 if total - largest >= count - 1 else 0
    counts, rest = [largest] + [least] * (count - 1), total - largest - least * (count - 1)
    while rest > 0:
        movable = [i for i in range(1, count) if counts[i] < largest] or [i for i in range(1, count) if counts[i] < limit]
        pool, budget = sum([loads[i] for i in movable]), rest
        for i in movable:
            addition = min(limit - counts[i], max(1, budget * loads[i] // pool), rest)
            counts[i] = counts[i] + addition
            rest = rest - addition
    return np.array(counts)


def normal_values(own_key, dims, deviation, limit, pieces=(), kind=jnp.bfloat16):
    entries = jax.random.normal(own_key, dims, jnp.float32) * deviation
    if len(pieces) > 0:
        entries = level_of(own_key, dims, pieces, -0.22, 0.18) * entries
    return jnp.clip(entries, min=-limit, max=limit).astype(kind)


def setup_inputs(seed: int = 0) -> dict:
    keys = jax.random.split(jax.random.key(seed), 11)
    tokens = normal_values(keys[0], (IMAGES, SEQ, D), 1.0, 6.0, ((0, 16), (1, 2)))
    gain_one = jnp.clip(1.0 + 0.18 * jax.random.normal(keys[1], (D,), jnp.float32), 0.1, 1.9)
    w_qkv = normal_values(keys[2], (D, 3 * D), D ** -0.5, 0.21875)
    w_out = normal_values(keys[3], (D, D), (max(D // 512, 1)) ** -0.5, 6.0)
    gain_two = jnp.clip(1.0 + 0.18 * jax.random.normal(keys[4], (D,), jnp.float32), 0.1, 1.9)
    w_router = normal_values(keys[5], (D, EXPERTS), (2 * D) ** -0.5, 0.15625)
    w_in = normal_values(keys[6], (EXPERTS, D, FF), D ** -0.5, 0.21875, ((0, 8),))
    w_back = normal_values(keys[7], (EXPERTS, FF, D), (max(FF // 256, 1)) ** -0.5, 1.75, ((0, 8),))
    expert_ids_keys = jax.random.split(jax.random.fold_in(keys[8], 1), N_CONTEXT * IMAGES * TOK_CTX // TOK_DEV)
    expert_ids_turns = jax.random.permutation(jax.random.fold_in(keys[8], 3), N_CONTEXT * IMAGES * TOK_CTX // TOK_DEV)
    expert_ids = jax.vmap(lambda own, number: assign_block(jax.random.fold_in(keys[8], 2), own, number, TOK_DEV, N_EXPERT, TOPK, CAP, 2))(expert_ids_keys, expert_ids_turns).reshape((N_CONTEXT, IMAGES, TOK_CTX, TOPK))
    cotangent = normal_values(keys[9], (IMAGES, SEQ, D), 1.0, 6.0, ((0, 16), (1, 2)))
    return {"tokens": tokens, "gain_one": gain_one, "w_qkv": w_qkv, "w_out": w_out, "gain_two": gain_two, "w_router": w_router, "w_in": w_in, "w_back": w_back, "expert_ids": expert_ids, "cotangent": cotangent}


@jax.custom_vjp
def low(v):
    return lax.optimization_barrier(v.astype(jnp.bfloat16)).astype(jnp.float32)

@jax.custom_vjp
def low_back(v):
    return v

def low_keep(v):
    return (low(v), None)

def low_pass(kept, grad):
    return (grad,)

def back_keep(v):
    return (v, None)

def back_low(kept, grad):
    return (low(grad),)
low.defvjp(low_keep, low_pass)
low_back.defvjp(back_keep, back_low)
finest = lax.Precision.HIGHEST

def layer_norm(values, gain):
    center = lax.optimization_barrier(jnp.mean(values, axis=-1, keepdims=True))
    shifted = values - center
    variance = lax.optimization_barrier(jnp.mean(shifted * shifted, axis=-1, keepdims=True))
    return shifted * lax.rsqrt(variance + 1e-06) * gain

def attend(packed_img):
    query = packed_img[:, :D].reshape(SEQ, HEADS, HEAD_DIM)
    keys_img = packed_img[:, D:2 * D].reshape(SEQ, HEADS, HEAD_DIM)
    vals_img = packed_img[:, 2 * D:].reshape(SEQ, HEADS, HEAD_DIM)
    raw = jnp.einsum('qhd,khd->hqk', query, keys_img, precision=finest)
    scores = low_back(raw) * HEAD_DIM ** (-0.5)
    probs = jax.nn.softmax(scores, axis=-1)
    mixed = jnp.einsum('hqk,khd->qhd', low(probs), vals_img, precision=finest)
    return mixed.reshape(SEQ, D)

def expert_rows(bundle):
    rows_in, weight_in, weight_back = bundle
    hidden = low_back(jnp.dot(rows_in, weight_in, precision=finest))
    active = low(jax.nn.gelu(hidden))
    return low(low_back(jnp.dot(active, weight_back, precision=finest)))

def reference(tokens, gain_one, w_qkv, w_out, gain_two, w_router, w_in, w_back, expert_ids, cotangent):
    nblocks = N_CONTEXT * IMAGES // IMG_DEV
    routes_blk = expert_ids.reshape(nblocks, TOK_DEV, TOPK).astype(jnp.int32)
    onehot = (routes_blk[..., None] == jnp.arange(EXPERTS, dtype=jnp.int32)).astype(jnp.int32)
    running = jnp.cumsum(onehot.reshape(nblocks, TOK_DEV * TOPK, EXPERTS), axis=1)
    running = running.reshape(nblocks, TOK_DEV, TOPK, EXPERTS)
    slot_pos = lax.optimization_barrier(jnp.sum(running * onehot, axis=-1)) - 1
    block_ids = jnp.arange(nblocks, dtype=jnp.int32)[:, None, None]
    row_ids = jnp.broadcast_to(jnp.arange(TOK_DEV, dtype=jnp.int32)[None, :, None], routes_blk.shape)
    table = jnp.zeros((EXPERTS, nblocks, CAP), jnp.int32).at[routes_blk, block_ids, slot_pos].set(row_ids)
    filled = jnp.zeros((EXPERTS, nblocks, CAP), jnp.float32).at[routes_blk, block_ids, slot_pos].set(1.0)
    block_grid = jnp.arange(nblocks, dtype=jnp.int32)[None, :, None]

    def to_blocks(values):
        split = values.reshape(IMAGES, N_CONTEXT, TOK_CTX, values.shape[-1]).transpose(1, 0, 2, 3)
        return split.reshape(nblocks, TOK_DEV, values.shape[-1])

    def from_blocks(values):
        split = values.reshape(N_CONTEXT, IMAGES, TOK_CTX, values.shape[-1]).transpose(1, 0, 2, 3)
        return split.reshape(IMAGES, SEQ, values.shape[-1])

    def forward(inputs, gain_a, weight_qkv, weight_out, gain_b, weight_router, weight_in, weight_back):
        normed = low(layer_norm(inputs, gain_a))
        packed = low(low_back(jnp.einsum('bsd,de->bse', normed, weight_qkv, precision=finest)))
        mixed = lax.map(jax.checkpoint(attend), packed)
        mixed = low(low_back(mixed))
        attn_out = low_back(jnp.einsum('bsd,de->bse', mixed, weight_out, precision=finest))
        resid = inputs + attn_out
        second = low(layer_norm(resid, gain_b))
        logits = low_back(jnp.einsum('bsd,de->bse', second, weight_router, precision=finest))
        gate_probs = jax.nn.softmax(logits, axis=-1)
        gates = jnp.take_along_axis(to_blocks(gate_probs), routes_blk, axis=-1)
        blocks = to_blocks(second)
        sent = low_back(blocks[block_grid, table] * filled[..., None])
        produced = lax.map(jax.checkpoint(expert_rows), (sent.reshape(EXPERTS, nblocks * CAP, D), weight_in, weight_back))
        produced = produced.reshape(EXPERTS, nblocks, CAP, D)
        picked = produced[routes_blk, block_ids, slot_pos]
        added = lax.optimization_barrier(jnp.sum(gates[..., None] * picked, axis=2))
        return resid + from_blocks(added)
    floats = (tokens.astype(jnp.float32), gain_one.astype(jnp.float32), w_qkv.astype(jnp.float32), w_out.astype(jnp.float32), gain_two.astype(jnp.float32), w_router.astype(jnp.float32), w_in.astype(jnp.float32), w_back.astype(jnp.float32))
    result, pullback = jax.vjp(forward, *floats)
    grads = pullback(cotangent.astype(jnp.float32))
    return (result.astype(jnp.bfloat16), grads[0], grads[1], grads[2], grads[3], grads[4], grads[5], grads[6], grads[7])
```

```python
import functools

import jax
import jax.numpy as jnp
from jax import lax
from jax.experimental import pallas as pl
from jax.experimental.pallas import tpu as pltpu
from jax.sharding import PartitionSpec as P

HEADS = 12
HEAD_DIM = 64
TOPK = 2
PAIR = 2 * HEAD_DIM
FACTOR = HEAD_DIM ** (-0.5)
LOW = jnp.bfloat16
FULL = jnp.float32
EVERY = ("expert", "context", "dp")
VMEM_LIMIT = 56 * 1024 * 1024


def layer_norm(values, gain):
    center = jnp.mean(values, axis=-1, keepdims=True)
    shifted = values - center
    variance = jnp.mean(shifted * shifted, axis=-1, keepdims=True)
    return shifted * lax.rsqrt(variance + 1e-06) * gain


def contract(left, right, left_dim, right_dim):
    return lax.dot_general(
        left, right, (((left_dim,), (right_dim,)), ((), ())), preferred_element_type=FULL
    )


def attend_kernel(query_ref, keys_ref, vals_ref, mixed_ref, lse_ref):
    parts = []
    for half in range(2):
        cols = slice(half * HEAD_DIM, (half + 1) * HEAD_DIM)
        query = query_ref[0, :, cols] * LOW(FACTOR)
        scores = contract(keys_ref[0, :, cols], query, 1, 1)
        peak = jnp.max(scores, axis=0, keepdims=True)
        expo = jnp.exp(scores - peak)
        total = jnp.sum(expo, axis=0, keepdims=True)
        lse_ref[0, 0, half : half + 1, :] = peak + jnp.log(total)
        parts.append(contract(vals_ref[0, :, cols], expo.astype(LOW), 0, 0) / total)
    mixed_ref[0] = jnp.concatenate(parts, axis=0).T.astype(LOW)


def attend(query, keys, vals):
    images, tok, width = query.shape
    seq = keys.shape[1]
    pairs = width // PAIR
    near = pl.BlockSpec((1, tok, PAIR), lambda i, p: (i, 0, p))
    whole = pl.BlockSpec((1, seq, PAIR), lambda i, p: (i, 0, p))
    return pl.pallas_call(
        attend_kernel,
        grid=(images, pairs),
        in_specs=[near, whole, whole],
        out_specs=[near, pl.BlockSpec((1, 1, 2, tok), lambda i, p: (i, p, 0, 0))],
        out_shape=[
            jax.ShapeDtypeStruct((images, tok, width), LOW),
            jax.ShapeDtypeStruct((images, pairs, 2, tok), FULL),
        ],
        compiler_params=pltpu.CompilerParams(vmem_limit_bytes=VMEM_LIMIT),
        cost_estimate=pl.CostEstimate(
            flops=4 * images * tok * seq * width,
            bytes_accessed=4 * images * (tok + seq) * width,
            transcendentals=images * tok * seq * HEADS,
        ),
        name="attend",
    )(query, keys, vals)


def attend_back_kernel(
    query_ref, keys_ref, vals_ref, up_ref, lse_ref, d_query_ref, d_keys_ref, d_vals_ref
):
    parts = []
    for half in range(2):
        cols = slice(half * HEAD_DIM, (half + 1) * HEAD_DIM)
        query = query_ref[0, :, cols] * LOW(FACTOR)
        keys = keys_ref[0, :, cols]
        up = up_ref[0, :, cols]
        probs = jnp.exp(contract(keys, query, 1, 1) - lse_ref[0, 0, half : half + 1, :])
        d_probs = contract(vals_ref[0, :, cols], up, 1, 1)
        delta = jnp.sum(probs * d_probs, axis=0, keepdims=True)
        d_scores = (probs * (d_probs - delta)).astype(LOW)
        d_vals_ref[0, :, cols] = contract(probs.astype(LOW), up, 1, 0).astype(LOW)
        d_keys_ref[0, :, cols] = contract(d_scores, query, 1, 0).astype(LOW)
        parts.append(contract(keys, d_scores, 0, 0) * FACTOR)
    d_query_ref[0] = jnp.concatenate(parts, axis=0).T.astype(LOW)


def attend_back(query, keys, vals, up, lse):
    images, tok, width = query.shape
    seq = keys.shape[1]
    pairs = width // PAIR
    near = pl.BlockSpec((1, tok, PAIR), lambda i, p: (i, 0, p))
    whole = pl.BlockSpec((1, seq, PAIR), lambda i, p: (i, 0, p))
    return pl.pallas_call(
        attend_back_kernel,
        grid=(images, pairs),
        in_specs=[near, whole, whole, near, pl.BlockSpec((1, 1, 2, tok), lambda i, p: (i, p, 0, 0))],
        out_specs=[near, whole, whole],
        out_shape=[
            jax.ShapeDtypeStruct((images, tok, width), LOW),
            jax.ShapeDtypeStruct((images, seq, width), LOW),
            jax.ShapeDtypeStruct((images, seq, width), LOW),
        ],
        compiler_params=pltpu.CompilerParams(vmem_limit_bytes=VMEM_LIMIT),
        cost_estimate=pl.CostEstimate(
            flops=10 * images * tok * seq * width,
            bytes_accessed=8 * images * (tok + seq) * width,
            transcendentals=images * tok * seq * HEADS,
        ),
        name="attend_back",
    )(query, keys, vals, up, lse)


def partners(axis, shift):
    return [(i, i ^ shift) for i in range(lax.axis_size(axis))]


def swap(block, axis, shift):
    return lax.ppermute(block, axis, partners(axis, shift)) if shift else block


def gather_near_first(block, axis):
    return [swap(block, axis, shift) for shift in range(lax.axis_size(axis))]


def scatter_sum(block, axis):
    size = block.shape[0] // lax.axis_size(axis)
    me = lax.axis_index(axis)
    total = None
    for shift in range(lax.axis_size(axis)):
        piece = lax.dynamic_slice_in_dim(block, (me ^ shift) * size, size, 0)
        piece = swap(piece, axis, shift).astype(FULL)
        total = piece if total is None else total + piece
    return total.astype(LOW)


def gather_in_order(block, axis):
    size = block.shape[0]
    me = lax.axis_index(axis)
    out = jnp.zeros((size * lax.axis_size(axis),) + block.shape[1:], block.dtype)
    for shift, piece in enumerate(gather_near_first(block, axis)):
        out = lax.dynamic_update_slice_in_dim(out, piece, (me ^ shift) * size, 0)
    return out


def sum_everywhere(part, order):
    high, wide = part.shape
    value = part.astype(LOW).reshape(high, 2, wide // 2).transpose(1, 0, 2)
    value = value.reshape(2 * high, wide // 2)
    for axis in order:
        value = scatter_sum(value, axis)
    for axis in order[::-1]:
        value = gather_in_order(value, axis)
    return value.reshape(2, high, wide // 2).transpose(1, 0, 2).reshape(high, wide).astype(FULL)


def expert_rows(arrived, up, w_router, weight_in, weight_back, mine):
    gate_probs = jax.nn.softmax(
        jnp.dot(arrived, w_router, preferred_element_type=FULL), axis=-1
    )
    column = (lax.broadcasted_iota(jnp.int32, gate_probs.shape, 1) == mine).astype(FULL)
    gate = jnp.sum(gate_probs * column, axis=-1, keepdims=True)
    hidden = jnp.dot(arrived, weight_in, preferred_element_type=FULL)
    active, gelu_back = jax.vjp(jax.nn.gelu, hidden)
    active_low = active.astype(LOW)
    produced = jnp.dot(active_low, weight_back, preferred_element_type=FULL)
    up_full = up.astype(FULL)
    d_gate = jnp.sum(up_full * produced, axis=-1)
    gated = (gate * produced).astype(LOW)
    d_produced = (gate * up_full).astype(LOW)
    d_active = contract(d_produced, weight_back, 1, 1)
    d_hidden = gelu_back(d_active)[0].astype(LOW)
    d_arrived = contract(d_hidden, weight_in, 1, 1).astype(LOW)
    return active_low, d_produced, d_hidden, gated, d_gate, d_arrived


def body(tokens, gain_one, w_qkv, w_out, gain_two, w_router, w_in, w_back, expert_ids, cotangent):
    images, tok_ctx, width = tokens.shape
    rows = images * tok_ctx
    experts = lax.axis_size("expert")
    mine = lax.axis_index("expert")
    capacity = max(2, 2 * TOPK * rows // experts)
    weight_in = w_in[0]
    weight_back = w_back[0]

    tokens_img = jnp.concatenate(gather_near_first(tokens, "context"), axis=1)

    routes = expert_ids.reshape(rows, TOPK).T
    owners = mine ^ lax.broadcasted_iota(jnp.int32, (experts, 1), 0)
    named = (routes[0][None] == owners) | (routes[1][None] == owners)
    place = jnp.where(named, jnp.cumsum(named.astype(jnp.int32), axis=1) - 1, -1)
    choose = (
        place[:, None, :] == lax.broadcasted_iota(jnp.int32, (experts, capacity, rows), 1)
    ).astype(LOW)
    far = experts // 2
    groups = (range(far), range(far, experts))

    def dispatch(values, group):
        chosen = choose[group.start : group.stop].reshape(-1, rows)
        sent = jnp.dot(chosen, values, preferred_element_type=FULL).astype(LOW)
        return [
            swap(sent[n * capacity : (n + 1) * capacity], "expert", shift)
            for n, shift in enumerate(group)
        ]

    def send_back(values, group):
        return [
            swap(values[n * capacity : (n + 1) * capacity], "expert", shift)
            for n, shift in enumerate(group)
        ]

    def collect(pieces):
        return contract(choose.reshape(-1, rows), jnp.concatenate(pieces, axis=0), 0, 0)

    up_rows = cotangent.reshape(rows, width)
    up_far = jnp.concatenate(dispatch(up_rows, groups[1]), axis=0)
    up_near = jnp.concatenate(dispatch(up_rows, groups[0]), axis=0)

    inputs = tokens.astype(FULL)
    normed, first_back = jax.vjp(layer_norm, inputs, gain_one)
    normed_low = normed.astype(LOW)
    query = jnp.einsum(
        "isd,de->ise", normed_low, w_qkv[:, :width], preferred_element_type=FULL
    ).astype(LOW)
    normed_img = layer_norm(tokens_img.astype(FULL), gain_one).astype(LOW)
    keys = jnp.einsum(
        "isd,de->ise", normed_img, w_qkv[:, width : 2 * width], preferred_element_type=FULL
    ).astype(LOW)
    vals = jnp.einsum(
        "isd,de->ise", normed_img, w_qkv[:, 2 * width :], preferred_element_type=FULL
    ).astype(LOW)
    mixed_low, lse = attend(query, keys, vals)
    attn_out = jnp.einsum("isd,de->ise", mixed_low, w_out, preferred_element_type=FULL)
    resid = inputs + attn_out
    second, second_back = jax.vjp(layer_norm, resid, gain_two)
    second_rows = second.astype(LOW).reshape(rows, width)

    arrived_far = jnp.concatenate(dispatch(second_rows, groups[1]), axis=0)
    arrived_near = jnp.concatenate(dispatch(second_rows, groups[0]), axis=0)
    act_n, dp_n, dh_n, gated_n, dg_n, da_n = expert_rows(
        arrived_near, up_near, w_router, weight_in, weight_back, mine
    )
    act_f, dp_f, dh_f, gated_f, dg_f, da_f = expert_rows(
        arrived_far, up_far, w_router, weight_in, weight_back, mine
    )
    d_rows_near = send_back(da_n, groups[0])
    d_rows_far = send_back(da_f, groups[1])
    d_gate_back = [
        swap(piece, "expert", shift)
        for shift, piece in enumerate(
            jnp.concatenate([dg_n, dg_f]).reshape(experts, -1, 128)
        )
    ]
    back_part = contract(act_n, dp_n, 0, 0) + contract(act_f, dp_f, 0, 0)
    in_part = contract(arrived_near, dh_n, 0, 0) + contract(arrived_far, dh_f, 0, 0)

    d_rows = collect(d_rows_near + d_rows_far)
    gated_f, gated_n, d_rows = lax.optimization_barrier((gated_f, gated_n, d_rows))
    added = collect(send_back(gated_n, groups[0]) + send_back(gated_f, groups[1]))
    output = (resid + added.reshape(images, tok_ctx, width)).astype(LOW)
    gate_probs = jax.nn.softmax(
        jnp.dot(second_rows, w_router, preferred_element_type=FULL), axis=-1
    )
    d_gate_slots = jnp.stack(d_gate_back).reshape(experts, capacity)
    d_gate_tok = jnp.sum(choose.astype(FULL) * d_gate_slots[:, :, None], axis=1)
    to_column = (owners == lax.broadcasted_iota(jnp.int32, (experts, experts), 1)).astype(FULL)
    d_probs = jnp.sum(d_gate_tok[:, :, None] * to_column[:, None, :], axis=0)
    d_logits = gate_probs * (d_probs - jnp.sum(gate_probs * d_probs, axis=-1, keepdims=True))
    d_logits_low = d_logits.astype(LOW)
    router_part = contract(second_rows, d_logits_low, 0, 0)
    d_second = d_rows + contract(d_logits_low, w_router, 1, 1)
    d_resid_norm, gain_two_part = second_back(d_second.reshape(images, tok_ctx, width))
    d_resid = cotangent.astype(FULL) + d_resid_norm
    d_attn = d_resid.astype(LOW)
    grad_of = functools.partial(jnp.einsum, "isd,ise->de", preferred_element_type=FULL)
    d_mixed = jnp.einsum("ise,de->isd", d_attn, w_out, preferred_element_type=FULL).astype(LOW)

    d_query, d_keys_img, d_vals_img = attend_back(query, keys, vals, d_mixed, lse)

    def sum_context(part):
        total = None
        for shift in range(lax.axis_size("context")):
            piece = swap(part[:, shift * tok_ctx : (shift + 1) * tok_ctx], "context", shift)
            total = piece.astype(FULL) if total is None else total + piece.astype(FULL)
        return total.astype(LOW)

    d_keys = sum_context(d_keys_img)
    d_vals = sum_context(d_vals_img)
    grad_out = sum_everywhere(grad_of(mixed_low, d_attn), ("dp", "context", "expert"))
    grad_v = sum_everywhere(grad_of(normed_img, d_vals_img), ("dp", "context", "expert"))
    grad_k = sum_everywhere(grad_of(normed_img, d_keys_img), ("dp", "expert", "context"))
    grad_q = sum_everywhere(grad_of(normed_low, d_query), ("context", "dp", "expert"))
    d_packed = jnp.concatenate([d_query, d_keys, d_vals], axis=-1)
    d_normed = jnp.einsum("ise,de->isd", d_packed, w_qkv, preferred_element_type=FULL)
    d_inputs_norm, gain_one_part = first_back(d_normed)
    grad_tokens = d_resid + d_inputs_norm
    grad_router, grad_gain_one, grad_gain_two = lax.psum(
        (router_part, gain_one_part, gain_two_part), EVERY
    )
    grad_in, grad_back = (
        lax.psum_scatter(
            part[None].astype(LOW), ("context", "dp"), scatter_dimension=1, tiled=True
        ).astype(FULL)
        for part in (in_part, back_part)
    )
    return (
        output,
        grad_tokens,
        grad_gain_one,
        jnp.concatenate([grad_q, grad_k, grad_v], axis=-1),
        grad_out,
        grad_gain_two,
        grad_router,
        grad_in,
        grad_back,
    )


def solution(mesh):
    return jax.shard_map(
        body,
        mesh=mesh,
        in_specs=(
            P(("expert", "dp"), "context", None),
            P(),
            P(),
            P(),
            P(),
            P(),
            P("expert", None, None),
            P("expert", None, None),
            P("context", ("expert", "dp"), None, None),
            P(("expert", "dp"), "context", None),
        ),
        out_specs=(
            P(("expert", "dp"), "context", None),
            P(("expert", "dp"), "context", None),
            P(),
            P(),
            P(),
            P(),
            P(),
            P("expert", ("context", "dp"), None),
            P("expert", ("context", "dp"), None),
        ),
        check_vma=False,
    )
```

```python
import functools

import jax
import jax.numpy as jnp
from jax import lax
from jax.experimental import pallas as pl
from jax.experimental.pallas import tpu as pltpu
from jax.sharding import PartitionSpec as P

HEADS = 12
HEAD_DIM = 64
TOPK = 2
PAIR = 2 * HEAD_DIM
FACTOR = HEAD_DIM ** (-0.5)
LOW = jnp.bfloat16
FULL = jnp.float32
EVERY = ("expert", "context", "dp")
VMEM_LIMIT = 56 * 1024 * 1024


def layer_norm(values, gain):
    center = jnp.mean(values, axis=-1, keepdims=True)
    shifted = values - center
    variance = jnp.mean(shifted * shifted, axis=-1, keepdims=True)
    return shifted * lax.rsqrt(variance + 1e-06) * gain


def contract(left, right, left_dim, right_dim):
    return lax.dot_general(
        left, right, (((left_dim,), (right_dim,)), ((), ())), preferred_element_type=FULL
    )


def attend_kernel(query_ref, keys_ref, vals_ref, mixed_ref, lse_ref):
    parts = []
    for half in range(2):
        cols = slice(half * HEAD_DIM, (half + 1) * HEAD_DIM)
        query = query_ref[0, :, cols] * LOW(FACTOR)
        scores = contract(keys_ref[0, :, cols], query, 1, 1)
        peak = jnp.max(scores, axis=0, keepdims=True)
        expo = jnp.exp(scores - peak)
        total = jnp.sum(expo, axis=0, keepdims=True)
        lse_ref[0, 0, half : half + 1, :] = peak + jnp.log(total)
        parts.append(contract(vals_ref[0, :, cols], expo.astype(LOW), 0, 0) / total)
    mixed_ref[0] = jnp.concatenate(parts, axis=0).T.astype(LOW)


def attend(query, keys, vals):
    images, tok, width = query.shape
    seq = keys.shape[1]
    pairs = width // PAIR
    near = pl.BlockSpec((1, tok, PAIR), lambda i, p: (i, 0, p))
    whole = pl.BlockSpec((1, seq, PAIR), lambda i, p: (i, 0, p))
    return pl.pallas_call(
        attend_kernel,
        grid=(images, pairs),
        in_specs=[near, whole, whole],
        out_specs=[near, pl.BlockSpec((1, 1, 2, tok), lambda i, p: (i, p, 0, 0))],
        out_shape=[
            jax.ShapeDtypeStruct((images, tok, width), LOW),
            jax.ShapeDtypeStruct((images, pairs, 2, tok), FULL),
        ],
        compiler_params=pltpu.CompilerParams(vmem_limit_bytes=VMEM_LIMIT),
        cost_estimate=pl.CostEstimate(
            flops=4 * images * tok * seq * width,
            bytes_accessed=4 * images * (tok + seq) * width,
            transcendentals=images * tok * seq * HEADS,
        ),
        name="attend",
    )(query, keys, vals)


def attend_back_kernel(
    query_ref, keys_ref, vals_ref, up_ref, lse_ref, d_query_ref, d_keys_ref, d_vals_ref
):
    parts = []
    for half in range(2):
        cols = slice(half * HEAD_DIM, (half + 1) * HEAD_DIM)
        query = query_ref[0, :, cols] * LOW(FACTOR)
        keys = keys_ref[0, :, cols]
        up = up_ref[0, :, cols]
        probs = jnp.exp(contract(keys, query, 1, 1) - lse_ref[0, 0, half : half + 1, :])
        d_probs = contract(vals_ref[0, :, cols], up, 1, 1)
        delta = jnp.sum(probs * d_probs, axis=0, keepdims=True)
        d_scores = (probs * (d_probs - delta)).astype(LOW)
        d_vals_ref[0, :, cols] = contract(probs.astype(LOW), up, 1, 0).astype(LOW)
        d_keys_ref[0, :, cols] = contract(d_scores, query, 1, 0).astype(LOW)
        parts.append(contract(keys, d_scores, 0, 0) * FACTOR)
    d_query_ref[0] = jnp.concatenate(parts, axis=0).T.astype(LOW)


def attend_back(query, keys, vals, up, lse):
    images, tok, width = query.shape
    seq = keys.shape[1]
    pairs = width // PAIR
    near = pl.BlockSpec((1, tok, PAIR), lambda i, p: (i, 0, p))
    whole = pl.BlockSpec((1, seq, PAIR), lambda i, p: (i, 0, p))
    return pl.pallas_call(
        attend_back_kernel,
        grid=(images, pairs),
        in_specs=[near, whole, whole, near, pl.BlockSpec((1, 1, 2, tok), lambda i, p: (i, p, 0, 0))],
        out_specs=[near, whole, whole],
        out_shape=[
            jax.ShapeDtypeStruct((images, tok, width), LOW),
            jax.ShapeDtypeStruct((images, seq, width), LOW),
            jax.ShapeDtypeStruct((images, seq, width), LOW),
        ],
        compiler_params=pltpu.CompilerParams(vmem_limit_bytes=VMEM_LIMIT),
        cost_estimate=pl.CostEstimate(
            flops=10 * images * tok * seq * width,
            bytes_accessed=8 * images * (tok + seq) * width,
            transcendentals=images * tok * seq * HEADS,
        ),
        name="attend_back",
    )(query, keys, vals, up, lse)


def partners(axis, shift):
    return [(i, i ^ shift) for i in range(lax.axis_size(axis))]


def swap(block, axis, shift):
    return lax.ppermute(block, axis, partners(axis, shift)) if shift else block


def gather_near_first(block, axis):
    return [swap(block, axis, shift) for shift in range(lax.axis_size(axis))]


def bits_of(axis):
    size, bits = lax.axis_size(axis), []
    while size > 1:
        size //= 2
        bits.append((axis, size))
    return bits


def halve(value, axis, bit):
    size = value.shape[0] // 2
    high = (lax.axis_index(axis) // bit) % 2
    kept = lax.dynamic_slice_in_dim(value, high * size, size, 0)
    given = lax.dynamic_slice_in_dim(value, (1 - high) * size, size, 0)
    return (kept.astype(FULL) + swap(given, axis, bit).astype(FULL)).astype(LOW)


def double(value, axis, bit):
    high = (lax.axis_index(axis) // bit) % 2
    other = swap(value, axis, bit)
    return jnp.concatenate(
        [jnp.where(high == 0, value, other), jnp.where(high == 0, other, value)], axis=0
    )


def sum_everywhere(part, order):
    high, wide = part.shape
    strip = 384
    value = part.astype(LOW).reshape(high, wide // strip, strip).transpose(1, 0, 2)
    value = value.reshape(-1, strip)
    for axis, bit in order:
        value = halve(value, axis, bit)
    for axis, bit in order[::-1]:
        value = double(value, axis, bit)
    value = value.reshape(wide // strip, high, strip).transpose(1, 0, 2)
    return value.reshape(high, wide).astype(FULL)


def sum_small(value, order):
    for axis, bit in order:
        value = value + swap(value, axis, bit)
    return value


def body(tokens, gain_one, w_qkv, w_out, gain_two, w_router, w_in, w_back, expert_ids, cotangent):
    images, tok_ctx, width = tokens.shape
    rows = images * tok_ctx
    experts = lax.axis_size("expert")
    mine = lax.axis_index("expert")
    capacity = max(2, 2 * TOPK * rows // experts)
    weight_in = w_in[0]
    weight_back = w_back[0]

    tokens_img = jnp.concatenate(gather_near_first(tokens, "context"), axis=1)

    routes = expert_ids.reshape(rows, TOPK).T
    owners = lax.broadcasted_iota(jnp.int32, (experts, 1), 0)
    named = (routes[0][None] == owners) | (routes[1][None] == owners)
    place = jnp.where(named, jnp.cumsum(named.astype(jnp.int32), axis=1) - 1, -1)
    taken = place[:, None, :] == lax.broadcasted_iota(jnp.int32, (experts, capacity, rows), 1)
    choose = taken.astype(LOW).reshape(-1, rows)

    def exchange(values):
        return lax.all_to_all(
            values.reshape(experts, capacity, width), "expert", 0, 0, tiled=True
        ).reshape(-1, width)

    def dispatch(values):
        return exchange(jnp.dot(choose, values, preferred_element_type=FULL).astype(LOW))

    up_rows = cotangent.reshape(rows, width)
    arrived_up = dispatch(up_rows)

    inputs = tokens.astype(FULL)
    normed, first_back = jax.vjp(layer_norm, inputs, gain_one)
    normed_low = normed.astype(LOW)
    query = jnp.einsum(
        "isd,de->ise", normed_low, w_qkv[:, :width], preferred_element_type=FULL
    ).astype(LOW)
    normed_img = layer_norm(tokens_img.astype(FULL), gain_one).astype(LOW)
    keys = jnp.einsum(
        "isd,de->ise", normed_img, w_qkv[:, width : 2 * width], preferred_element_type=FULL
    ).astype(LOW)
    vals = jnp.einsum(
        "isd,de->ise", normed_img, w_qkv[:, 2 * width :], preferred_element_type=FULL
    ).astype(LOW)
    mixed_low, lse = attend(query, keys, vals)
    attn_out = jnp.einsum("isd,de->ise", mixed_low, w_out, preferred_element_type=FULL)
    resid = inputs + attn_out
    second, second_back = jax.vjp(layer_norm, resid, gain_two)
    second_rows = second.astype(LOW).reshape(rows, width)

    second_rows, arrived_up = lax.optimization_barrier((second_rows, arrived_up))
    arrived = dispatch(second_rows)
    hidden = jnp.dot(arrived, weight_in, preferred_element_type=FULL)
    active_low = jax.nn.gelu(hidden).astype(LOW)
    produced = jnp.dot(active_low, weight_back, preferred_element_type=FULL).astype(LOW)
    returned = exchange(produced)
    arrived_probs = jax.nn.softmax(
        jnp.dot(arrived, w_router, preferred_element_type=FULL), axis=-1
    )
    column = (lax.broadcasted_iota(jnp.int32, arrived_probs.shape, 1) == mine).astype(FULL)
    arrived_gate = jnp.sum(arrived_probs * column, axis=-1, keepdims=True)
    d_produced = (arrived_gate * arrived_up.astype(FULL)).astype(LOW)
    d_active = contract(d_produced, weight_back, 1, 1)
    _, gelu_back = jax.vjp(jax.nn.gelu, hidden)
    d_hidden = gelu_back(d_active)[0].astype(LOW)
    d_arrived = contract(d_hidden, weight_in, 1, 1).astype(LOW)
    d_arrived, returned, active_low, d_produced, arrived, d_hidden = lax.optimization_barrier(
        (d_arrived, returned, active_low, d_produced, arrived, d_hidden)
    )
    returned_grad = exchange(d_arrived)
    back_part = contract(active_low, d_produced, 0, 0)
    in_part = contract(arrived, d_hidden, 0, 0)

    gate_probs = jax.nn.softmax(
        jnp.dot(second_rows, w_router, preferred_element_type=FULL), axis=-1
    )
    weighted = jnp.where(taken, gate_probs.T[:, None, :], 0.0).astype(LOW).reshape(-1, rows)
    added = contract(weighted, returned, 0, 0)
    output = (resid + added.reshape(images, tok_ctx, width)).astype(LOW)
    met = contract(returned, up_rows, 1, 1).reshape(experts, capacity, rows)
    d_probs = jnp.sum(jnp.where(taken, met, 0.0), axis=1).T
    d_rows = contract(choose, returned_grad, 0, 0)
    d_logits = gate_probs * (d_probs - jnp.sum(gate_probs * d_probs, axis=-1, keepdims=True))
    d_logits_low = d_logits.astype(LOW)
    router_part = contract(second_rows, d_logits_low, 0, 0)
    d_second = d_rows + contract(d_logits_low, w_router, 1, 1)
    d_resid_norm, gain_two_part = second_back(d_second.reshape(images, tok_ctx, width))
    d_resid = cotangent.astype(FULL) + d_resid_norm
    d_attn = d_resid.astype(LOW)
    grad_of = functools.partial(jnp.einsum, "isd,ise->de", preferred_element_type=FULL)
    d_mixed = jnp.einsum("ise,de->isd", d_attn, w_out, preferred_element_type=FULL).astype(LOW)

    d_query, d_keys_img, d_vals_img = attend_back(query, keys, vals, d_mixed, lse)

    def sum_context(part):
        total = None
        for shift in range(lax.axis_size("context")):
            piece = swap(part[:, shift * tok_ctx : (shift + 1) * tok_ctx], "context", shift)
            total = piece.astype(FULL) if total is None else total + piece.astype(FULL)
        return total.astype(LOW)

    d_keys = sum_context(d_keys_img)
    d_vals = sum_context(d_vals_img)
    bits_e, bits_c, bits_d = bits_of("expert"), bits_of("context"), bits_of("dp")
    plain = bits_d + bits_c + bits_e[::-1]
    turned = bits_d + bits_e[::-1][:1] + bits_c + bits_e[::-1][1:]
    grad_out = sum_everywhere(grad_of(mixed_low, d_attn), plain)
    grad_v = sum_everywhere(grad_of(normed_img, d_vals_img), plain)
    grad_qk = sum_everywhere(
        jnp.concatenate(
            [grad_of(normed_low, d_query), grad_of(normed_img, d_keys_img)], axis=-1
        ),
        turned,
    )
    d_packed = jnp.concatenate([d_query, d_keys, d_vals], axis=-1)
    d_normed = jnp.einsum("ise,de->isd", d_packed, w_qkv, preferred_element_type=FULL)
    d_inputs_norm, gain_one_part = first_back(d_normed)
    grad_tokens = d_resid + d_inputs_norm
    small = jnp.concatenate([router_part.reshape(-1), gain_one_part, gain_two_part])
    small = sum_small(small.reshape(-1, 128), plain).reshape(-1)
    grad_router = small[: -2 * width].reshape(width, experts)
    grad_gain_one = small[-2 * width : -width]
    grad_gain_two = small[-width:]
    grad_in, grad_back = (
        lax.psum_scatter(
            part[None].astype(LOW), ("context", "dp"), scatter_dimension=1, tiled=True
        ).astype(FULL)
        for part in (in_part, back_part)
    )
    return (
        output,
        grad_tokens,
        grad_gain_one,
        jnp.concatenate([grad_qk, grad_v], axis=-1),
        grad_out,
        grad_gain_two,
        grad_router,
        grad_in,
        grad_back,
    )


def solution(mesh):
    return jax.shard_map(
        body,
        mesh=mesh,
        in_specs=(
            P(("expert", "dp"), "context", None),
            P(),
            P(),
            P(),
            P(),
            P(),
            P("expert", None, None),
            P("expert", None, None),
            P("context", ("expert", "dp"), None, None),
            P(("expert", "dp"), "context", None),
        ),
        out_specs=(
            P(("expert", "dp"), "context", None),
            P(("expert", "dp"), "context", None),
            P(),
            P(),
            P(),
            P(),
            P(),
            P("expert", ("context", "dp"), None),
            P("expert", ("context", "dp"), None),
        ),
        check_vma=False,
    )
```
